32 devices in a mesh: groups: 2 (over y), occ: 4 (over z), aux: 4 (over x, core).
Axes of the slice: x: 2, y: 2, z: 4, core: 2. Of those that a mesh axis runs over, the one named last changes fastest.
Arguments:
- b_tensor: float32 [8, 2560, 1800], P(('groups', 'occ'), 'aux'), parts along dimension 0, may hold values from -2 to 2
- eps_occ: float32 [8], P(('groups', 'occ')), parts along dimension 0, may hold values from -2 to -0.3
- eps_virt: float32 [3600], P('groups'), parts along dimension 0, may hold values from 0.2 to 4
Outputs:
- gamma: float32 [8, 2560, 64], P(('groups', 'occ'), 'aux'), parts along dimension 0
- pair_energy: float32 [8, 2], P(('groups', 'occ')), parts along dimension 0
The draws below stay inside these ranges and needn't reach their ends.
There are 2 independent parts, one for each index of `groups`. The reference program is written for one: setup_inputs(seed, part) draws one part's arguments, and reference() takes and returns one part's arrays. A program takes and returns all parts, laid end to end along the dimension named above; each array names one. Nothing has to cross between parts.
All inputs are finite; a program needn't handle non-finite values.
Results may differ from the reference program's by a relative error of at most 0.0003.
Values sent between devices are 32-bit elements; how exact they have to be, the bound alone decides.
A program may use at most 64 MiB of HBM per device.

```python
import math
import jax
import jax.numpy as jnp
from jax import lax

NV = 1800
VB = 64
NOCC = 4
NAUX = 2560


def block_scale(rng, shape, shards, least, largest):
    loudness, own = 1.0, jax.random.fold_in(rng, 6)
    for position, blocks in shards:
        draws = jnp.exp(jax.random.uniform(jax.random.fold_in(own, position), (blocks,), jnp.float32, least / len(shards), largest / len(shards)))
        loudness = loudness * jnp.repeat(draws, shape[position] // blocks).reshape([-1 if axis == position else 1 for axis in range(len(shape))])
    return loudness


def bell_draw(stream_key, dims, spread, limit, shards=(), held_as=jnp.bfloat16):
    level = block_scale(stream_key, dims, shards, -0.22, 0.18) if shards else 1.0
    result = jax.random.normal(stream_key, dims, jnp.float32) * spread * level
    return jnp.minimum(jnp.maximum(result, -limit), limit).astype(held_as)


def setup_inputs(seed: int = 0, part: int = 0) -> dict:
    splits = jax.random.split(jax.random.key(seed), 4)
    part_keys = jax.random.split(jax.random.fold_in(splits[3], part), 4)
    return {
        "b_tensor": bell_draw(part_keys[0], (NOCC, NAUX, NV), (NAUX ** -0.25), 2.0, ((0, 4), (1, 4)), jnp.float32),
        "eps_occ": jnp.clip(-2.0 + 1.7 * jax.random.uniform(part_keys[1], (NOCC,), jnp.float32) ** block_scale(part_keys[1], (NOCC,), ((0, 4),), -0.2, 0.2), -2.0, -0.3),
        "eps_virt": jnp.clip(jnp.exp(jax.random.uniform(part_keys[2], (NV,), jnp.float32, math.log(0.2), math.log(4.0))), 0.2, 4.0),
    }


def reference(b_tensor, eps_occ, eps_virt):
    hp = lax.Precision.HIGHEST

    def one_orbital(index):
        own = b_tensor[index]
        e_own = eps_occ[index]
        total = jnp.zeros((NAUX, VB), jnp.float32)
        energies = []
        for offset in (1, 2):
            other_index = (index - offset) % NOCC
            other = b_tensor[other_index]
            e_other = eps_occ[other_index]
            coul = jnp.einsum("qa,qb->ab", own[:, :VB], other, precision=hp)
            exch = jnp.einsum("qa,qb->ab", other[:, :VB], own, precision=hp)
            denom = eps_virt[:VB, None] + eps_virt[None, :] - e_own - e_other
            amp = (2.0 * coul - exch) / denom
            energies.append(jnp.sum(coul * amp))
            total = total + jnp.einsum("qb,ab->qa", other, amp, precision=hp)
        return total, jnp.stack(energies)

    gamma, pair_energy = lax.map(one_orbital, jnp.arange(NOCC, dtype=jnp.int32))
    return gamma, pair_energy
```

```python
import functools

import jax
import jax.numpy as jnp
from jax import lax
from jax.experimental import pallas as pl
from jax.experimental.pallas import tpu as pltpu
from jax.sharding import PartitionSpec as P

VB = 64
CHUNKS = 3
MESH = pl.DeviceIdType.MESH
F32 = jnp.float32
BF16 = jnp.bfloat16


def split(x):
    hi = x.astype(BF16)
    return hi, (x - hi.astype(F32)).astype(BF16)


def dot(x, y):
    return lax.dot_general(x, y, (((1,), (0,)), ((), ())), preferred_element_type=F32)


def dot_t(x, y):
    return lax.dot_general(x, y, (((1,), (1,)), ((), ())), preferred_element_type=F32)


def distinct(n):
    return sorted({1 % n, 2 % n, (n - 1) % n, (n - 2) % n} - {0})


def kernel(n, levels, chunks, nv, *refs):
    b_hbm, eo_ref, ev_ref, gout, eout = refs[:5]
    (first, bv, bhi, blo, st, srecv, a1, evp, evc, esend, eocc, amp, ex, eacc,
     gacc, gsend, grecv, psend, precv) = refs[5:24]
    cur = refs[24:25 + levels]
    rec = refs[25 + levels:25 + 2 * levels]
    load_sem, send_sem, recv_sem = refs[25 + 2 * levels:]

    offs = distinct(n)
    ne = len(offs)
    rows_all = ne * VB
    depth, width = bhi.shape
    w = width // chunks
    me = lax.axis_index("occ")
    aux = lax.axis_index("aux")
    bits = [lax.rem(lax.div(aux, 2 ** level), 2) for level in range(levels)]
    buddy = [aux + (1 - 2 * bits[level]) * 2 ** level for level in range(levels)]
    rows = VB >> levels

    starts = []
    lo = 0
    for level in range(levels):
        lo = lo + bits[level] * (VB >> (level + 1))
        starts.append(pl.multiple_of(lo, 8))
    lo = starts[-1]

    sends = []

    def occ_at(offset):
        return lax.rem(me + offset, n)

    def push(src, dst, target):
        k = len(sends)
        copy = pltpu.make_async_remote_copy(
            src_ref=src, dst_ref=dst, send_sem=send_sem.at[k], recv_sem=recv_sem.at[k],
            device_id=target, device_id_type=MESH)
        copy.start()
        sends.append(copy)
        return copy

    load_first = pltpu.make_async_copy(b_hbm.at[0, :, pl.ds(0, 128)], first, load_sem.at[0])
    load_first.start()
    load_all = pltpu.make_async_copy(b_hbm.at[0], bv, load_sem.at[1])
    load_all.start()

    barrier = pltpu.get_barrier_semaphore()
    for offset in offs:
        pl.semaphore_signal(barrier, inc=1, device_id={"occ": occ_at(offset)}, device_id_type=MESH)
    for level in range(levels):
        pl.semaphore_signal(barrier, inc=1, device_id={"aux": buddy[level]}, device_id_type=MESH)

    esend[...] = jnp.full((8, 128), eo_ref[0], F32)
    load_first.wait()
    st[...] = first[...].T[:VB]
    pl.semaphore_wait(barrier, ne + levels)

    s_copies = [push(st, srecv.at[k], {"occ": occ_at(n - offset)}) for k, offset in enumerate(offs)]
    e_copies = [push(esend, eocc.at[k - 1], {"occ": occ_at(n - k)}) for k in (1, 2)]

    evp[...] = jnp.ones_like(evp)
    evp[:, :nv] = ev_ref[...]
    evc[...] = jnp.broadcast_to(evp[:, :128], (128, 128)).T
    eacc[...] = jnp.zeros_like(eacc)
    bhi[:, width - 128:] = jnp.zeros((depth, 128), BF16)
    blo[:, width - 128:] = jnp.zeros((depth, 128), BF16)
    load_all.wait()

    @pl.loop(0, depth // 16)
    def _(t):
        block = pl.ds(pl.multiple_of(t * 16, 16), 16)
        hi, low = split(bv[block, :])
        bhi[block, :nv] = hi
        blo[block, :nv] = low

    for k in range(ne):
        s_copies[k].wait_recv()
        hi, low = split(srecv[k])
        a1[k * VB:(k + 1) * VB, :] = hi
        a1[rows_all + k * VB:rows_all + (k + 1) * VB, :] = low
    for copy in e_copies:
        copy.wait_recv()

    flying = {}

    def start_level(level, c):
        cols = pl.ds(c * w, w)
        half = VB >> (level + 1)
        away = pl.multiple_of((1 - bits[level]) * half, 8)
        flying["rs", level, c] = push(
            cur[level].at[:, pl.ds(away, half), cols], rec[level].at[:, :, cols], {"aux": buddy[level]})

    def start_gather(level, c):
        cols = pl.ds(c * w, w)
        block = amp.at[:, pl.ds(starts[level], VB >> (level + 1)), cols]
        flying["ag", level, c] = push(block, block, {"aux": buddy[level]})

    def products(c):
        cols = slice(c * w, (c + 1) * w)
        t = dot(a1[...], bhi[:, cols])
        u = dot(a1[:rows_all, :], blo[:, cols])
        cur[0][:, :, cols] = (t[:rows_all] + t[rows_all:] + u).reshape(ne, VB, w)
        start_level(0, c)

    def reduce_level(level, c):
        cols = slice(c * w, (c + 1) * w)
        half = VB >> (level + 1)
        flying["rs", level, c].wait_recv()
        keep = pl.multiple_of(bits[level] * half, 8)
        cur[level + 1][:, :, cols] = cur[level][:, pl.ds(keep, half), cols] + rec[level][:, :, cols]
        if level + 1 < levels:
            start_level(level + 1, c)
        else:
            for k in (1, 2):
                flying["ex", k, c] = push(
                    cur[levels].at[offs.index(n - k), :, pl.ds(c * w, w)],
                    ex.at[k - 1, :, pl.ds(c * w, w)], {"occ": occ_at(n - k)})

    def amplitudes(c):
        cols = slice(c * w, (c + 1) * w)
        for k in (1, 2):
            flying["ex", k, c].wait_recv()
            coul = cur[levels][offs.index(k), :, cols]
            exch = ex[k - 1, :, cols]
            base = evc[pl.ds(lo, rows), 0:1] - eocc[k - 1, 0:1, 0:1] - esend[0:1, 0:1]
            val = (2.0 * coul - exch) / (base + evp[:, cols])
            prod = coul * val
            part = eacc[k - 1]
            for t in range(w // 128):
                part = part + prod[:, t * 128:(t + 1) * 128]
            eacc[k - 1] = part
            if c == chunks - 1:
                column = lax.broadcasted_iota(jnp.int32, (rows, w), 1) + c * w
                val = jnp.where(column < nv, val, jnp.sum(part, axis=1, keepdims=True))
            amp[k - 1, pl.ds(lo, rows), cols] = val
        start_gather(levels - 1, c)

    def gather_level(level, c):
        flying["ag", level, c].wait_recv()
        start_gather(level - 1, c)

    final = []

    def gammas(c):
        cols = slice(c * w, (c + 1) * w)
        flying["ag", 0, c].wait_recv()
        if c == chunks - 1:
            for k in (1, 2):
                total = jnp.sum(amp[k - 1, :, width - 128:], axis=0, keepdims=True)
                psend[k - 1] = jnp.broadcast_to(total[:, 127:128], (8, 128))
                final.append(push(psend.at[k - 1], precv.at[k - 1], {"occ": occ_at(k)}))
        hi, low = split(amp[:, :, cols].reshape(2 * VB, w))
        t = dot_t(bhi[:, cols], jnp.concatenate([hi, low], axis=0))
        u = dot_t(blo[:, cols], hi)
        part = t[:, :2 * VB] + t[:, 2 * VB:] + u
        gacc[...] = part if c == 0 else gacc[...] + part

    stages = [products]
    stages += [functools.partial(reduce_level, level) for level in range(levels)]
    stages += [amplitudes]
    stages += [functools.partial(gather_level, level) for level in range(levels - 1, 0, -1)]
    stages += [gammas]
    for t in range(chunks + len(stages) - 1):
        for s, stage in enumerate(stages):
            if 0 <= t - s < chunks:
                stage(t - s)

    gsend[...] = gacc[...].T.reshape(2, VB, depth)
    g_copies = [push(gsend.at[k - 1], grecv.at[k - 1], {"occ": occ_at(k)}) for k in (1, 2)]
    for copy in final:
        copy.wait_recv()
    lane = lax.broadcasted_iota(jnp.int32, (8, 128), 1)
    eout[...] = jnp.where(lane == 0, precv[0], precv[1])[0:1, 0:2]
    for copy in g_copies:
        copy.wait_recv()
    gout[...] = grecv[0] + grecv[1]
    for copy in sends:
        copy.wait_send()


def body(n, m, b_tensor, eps_occ, eps_virt):
    _, depth, nv = b_tensor.shape
    width = (nv // 128 + 1) * 128
    levels = m.bit_length() - 1
    ne = len(distinct(n))
    tiles = width // 128
    chunks = CHUNKS if tiles % CHUNKS == 0 else 1
    rows = VB >> levels
    scratch = [
        pltpu.VMEM((depth, 128), F32),
        pltpu.VMEM((depth, nv), F32),
        pltpu.VMEM((depth, width), BF16),
        pltpu.VMEM((depth, width), BF16),
        pltpu.VMEM((VB, depth), F32),
        pltpu.VMEM((ne, VB, depth), F32),
        pltpu.VMEM((2 * ne * VB, depth), BF16),
        pltpu.VMEM((1, width), F32),
        pltpu.VMEM((128, 128), F32),
        pltpu.VMEM((8, 128), F32),
        pltpu.VMEM((2, 8, 128), F32),
        pltpu.VMEM((2, VB, width), F32),
        pltpu.VMEM((2, rows, width), F32),
        pltpu.VMEM((2, rows, 128), F32),
        pltpu.VMEM((depth, 2 * VB), F32),
        pltpu.VMEM((2, VB, depth), F32),
        pltpu.VMEM((2, VB, depth), F32),
        pltpu.VMEM((2, 8, 128), F32),
        pltpu.VMEM((2, 8, 128), F32),
    ]
    scratch += [pltpu.VMEM((ne, VB >> level, width), F32) for level in range(levels + 1)]
    scratch += [pltpu.VMEM((ne, VB >> (level + 1), width), F32) for level in range(levels)]
    copies = ne + 2 + chunks * (2 * levels + 2) + 4
    scratch += [
        pltpu.SemaphoreType.DMA((2,)),
        pltpu.SemaphoreType.DMA((copies,)),
        pltpu.SemaphoreType.DMA((copies,)),
    ]
    flops = 6 * depth * width * VB * (ne + 2)
    gamma, energy = pl.pallas_call(
        functools.partial(kernel, n, levels, chunks, nv),
        out_shape=(jax.ShapeDtypeStruct((VB, depth), F32), jax.ShapeDtypeStruct((1, 2), F32)),
        in_specs=[
            pl.BlockSpec(memory_space=pl.ANY),
            pl.BlockSpec(memory_space=pltpu.SMEM),
            pl.BlockSpec(memory_space=pltpu.VMEM),
        ],
        out_specs=(pl.BlockSpec(memory_space=pltpu.VMEM), pl.BlockSpec(memory_space=pltpu.VMEM)),
        scratch_shapes=scratch,
        compiler_params=pltpu.CompilerParams(
            collective_id=0, has_side_effects=True, vmem_limit_bytes=48 * 2 ** 20),
        cost_estimate=pl.CostEstimate(flops=flops, bytes_accessed=4 * depth * nv, transcendentals=0),
    )(b_tensor, eps_occ, eps_virt.reshape(1, nv))
    return gamma.T[None], energy


def solution(mesh):
    placed = (P(("groups", "occ"), "aux", None), P(("groups", "occ")), P("groups"))
    return jax.shard_map(
        functools.partial(body, mesh.shape["occ"], mesh.shape["aux"]),
        mesh=mesh,
        in_specs=placed,
        out_specs=(P(("groups", "occ"), "aux", None), P(("groups", "occ"), None)),
        check_vma=False,
    )
```

```python
import functools

import jax
import jax.numpy as jnp
from jax import lax
from jax.experimental import pallas as pl
from jax.experimental.pallas import tpu as pltpu
from jax.sharding import PartitionSpec as P

VB = 64
PARTS = {1: 3, 2: 1}
VMEM_MIB = 60
MESH = pl.DeviceIdType.MESH
F32 = jnp.float32
BF16 = jnp.bfloat16


def split(x):
    hi = x.astype(BF16)
    return hi, (x - hi.astype(F32)).astype(BF16)


def dot(x, y):
    return lax.dot_general(x, y, (((1,), (0,)), ((), ())), preferred_element_type=F32)


def dot_t(x, y):
    return lax.dot_general(x, y, (((1,), (1,)), ((), ())), preferred_element_type=F32)


def near(n, k):
    return sorted({k % n, (n - k) % n})


def schedule(levels, parts):
    first = [(2, c) for c in range(parts[2])]
    later = [(1, c) for c in range(parts[1])]
    order = [("products", 0, piece) for piece in first]
    for level in range(levels):
        order += [("reduce", level, piece) for piece in first]
    stages = [("products", 0)] + [("reduce", level) for level in range(levels)] + [("amplitudes", 0)]
    stages += [("gather", level) for level in range(levels - 1, 0, -1)] + [("gammas", 0)]
    rest = [("amplitudes", 0)] + [("gather", level) for level in range(levels - 1, 0, -1)] + [("gammas", 0)]
    for t in range(len(later) + len(stages) - 1):
        for s, stage in enumerate(stages):
            if 0 <= t - s < len(later):
                order.append((*stage, later[t - s]))
        if t >= 1 and rest:
            stage = rest.pop(0)
            order += [(*stage, piece) for piece in first]
    for stage in rest:
        order += [(*stage, piece) for piece in first]
    return order


def kernel(n, levels, parts, nv, *refs):
    b_hbm, eo_ref, ev_ref, gout, eout = refs[:5]
    (bv, bhi, blo, srecv, ahi, evp, evc, esend, eocc, amp, ex, eacc,
     gsend, grecv, psend, precv) = refs[5:21]
    at = 21
    cur, rec = {}, {}
    for k in (1, 2):
        cur[k] = refs[at:at + levels + 1]
        rec[k] = refs[at + levels + 1:at + 2 * levels + 1]
        at += 2 * levels + 1
    load_sem, send_sem, recv_sem = refs[at:]

    offs = sorted(set(near(n, 1) + near(n, 2)))
    ne = len(offs)
    width, depth = bhi.shape
    me = lax.axis_index("occ")
    aux = lax.axis_index("aux")
    bits = [lax.rem(lax.div(aux, 2 ** level), 2) for level in range(levels)]
    buddy = [aux + (1 - 2 * bits[level]) * 2 ** level for level in range(levels)]
    rows = VB >> levels

    starts = []
    lo = 0
    for level in range(levels):
        lo = lo + bits[level] * (VB >> (level + 1))
        starts.append(pl.multiple_of(lo, 8))
    lo = starts[-1]

    sends = []

    def occ_at(offset):
        return lax.rem(me + offset, n)

    def push(src, dst, target, slot=None, when=None):
        k = len(sends)
        copy = pltpu.make_async_remote_copy(
            src_ref=src, dst_ref=dst, send_sem=send_sem.at[k],
            recv_sem=recv_sem.at[ne + k if slot is None else slot],
            device_id=target, device_id_type=MESH)
        if when is None:
            copy.start()
        else:
            pl.when(when)(copy.start)
        sends.append((copy, when))
        return copy

    barrier = pltpu.get_barrier_semaphore()
    for offset in offs:
        pl.semaphore_signal(barrier, inc=1, device_id={"occ": occ_at(offset)}, device_id_type=MESH)
    for level in range(levels):
        pl.semaphore_signal(barrier, inc=1, device_id={"aux": buddy[level]}, device_id_type=MESH)
    load = pltpu.make_async_copy(b_hbm.at[0], bv.at[pl.ds(0, nv), :], load_sem.at[0])
    load.start()
    esend[...] = jnp.full((8, 128), eo_ref[0], F32)
    pl.semaphore_wait(barrier, ne + levels)

    batch = b_hbm.at[0, pl.ds(0, VB), :]
    arrivals = {}

    def share(offset, when=None):
        slot = offs.index(offset)
        arrivals[offset] = push(batch, srecv.at[slot], {"occ": occ_at(n - offset)}, slot, when)

    for offset in near(n, 2):
        share(offset)
    e_copies = [push(esend, eocc.at[k - 1], {"occ": occ_at(n - k)}) for k in (2, 1)]
    if n == 4:
        share(1, me > 0)
        share(3, me < 3)
    else:
        for offset in near(n, 1):
            share(offset)

    evp[...] = jnp.ones_like(evp)
    evp[:, :nv] = ev_ref[...]
    evc[...] = jnp.broadcast_to(evp[:, :128], (128, 128)).T
    eacc[...] = jnp.zeros_like(eacc)
    bv[nv:, :] = jnp.zeros((width - nv, depth), F32)
    load.wait()

    @pl.loop(0, width // 16)
    def _(t):
        block = pl.ds(pl.multiple_of(t * 16, 16), 16)
        hi, low = split(bv[block, :])
        bhi[block, :] = hi
        blo[block, :] = low

    if n == 4:
        arrivals[2].wait_recv()
        passed = srecv.at[offs.index(2)]
        push(passed, srecv.at[offs.index(1)], {"occ": occ_at(1)}, offs.index(1), me == 2)
        push(passed, srecv.at[offs.index(3)], {"occ": occ_at(3)}, offs.index(3), me == 1)

    flying = {}

    def span(piece):
        k, c = piece
        w = width // parts[k]
        return slice(c * w, (c + 1) * w), pl.ds(c * w, w), w

    def start_level(level, piece):
        k, c = piece
        _, cols, _ = span(piece)
        half = VB >> (level + 1)
        away = pl.multiple_of((1 - bits[level]) * half, 8)
        flying["reduce", level, piece] = push(
            cur[k][level].at[:, pl.ds(away, half), cols], rec[k][level].at[:, :, cols],
            {"aux": buddy[level]})

    def start_gather(level, piece):
        k, c = piece
        _, cols, _ = span(piece)
        block = amp.at[k - 1, pl.ds(starts[level], VB >> (level + 1)), cols]
        flying["gather", level, piece] = push(block, block, {"aux": buddy[level]})

    def products(_, piece):
        k, c = piece
        mine = near(n, k)
        cols, _, w = span(piece)
        m = len(mine) * VB
        if c == 0:
            for s, offset in enumerate(mine):
                if not (n == 4 and offset == 2):
                    arrivals[offset].wait_recv()
                hi, low = split(srecv[offs.index(offset)])
                ahi[s * VB:(s + 1) * VB, :] = hi
                ahi[m + s * VB:m + (s + 1) * VB, :] = low
        t = dot_t(ahi[:2 * m, :], bhi[cols, :])
        u = dot_t(ahi[:m, :], blo[cols, :])
        cur[k][0][:, :, cols] = (t[:m] + t[m:] + u).reshape(len(mine), VB, w)
        start_level(0, piece)

    def reduce_level(level, piece):
        k, c = piece
        cols, dcols, _ = span(piece)
        half = VB >> (level + 1)
        flying["reduce", level, piece].wait_recv()
        keep = pl.multiple_of(bits[level] * half, 8)
        cur[k][level + 1][:, :, cols] = cur[k][level][:, pl.ds(keep, half), cols] + rec[k][level][:, :, cols]
        if level + 1 < levels:
            start_level(level + 1, piece)
        else:
            flying["ex", piece] = push(
                cur[k][levels].at[near(n, k).index(n - k), :, dcols],
                ex.at[k - 1, :, dcols], {"occ": occ_at(n - k)})

    def amplitudes(_, piece):
        k, c = piece
        cols, _, w = span(piece)
        if c == 0:
            e_copies[2 - k].wait_recv()
        flying["ex", piece].wait_recv()
        coul = cur[k][levels][near(n, k).index(k), :, cols]
        exch = ex[k - 1, :, cols]
        base = evc[pl.ds(lo, rows), 0:1] - eocc[k - 1, 0:1, 0:1] - esend[0:1, 0:1]
        val = (2.0 * coul - exch) / (base + evp[:, cols])
        prod = coul * val
        part = eacc[k - 1]
        for t in range(w // 128):
            part = part + prod[:, t * 128:(t + 1) * 128]
        eacc[k - 1] = part
        if c == parts[k] - 1:
            column = lax.broadcasted_iota(jnp.int32, (rows, w), 1) + c * w
            val = jnp.where(column < nv, val, jnp.sum(part, axis=1, keepdims=True))
        amp[k - 1, pl.ds(lo, rows), cols] = val
        start_gather(levels - 1, piece)

    def gather_level(level, piece):
        flying["gather", level, piece].wait_recv()
        start_gather(level - 1, piece)

    final = []

    def gammas(_, piece):
        k, c = piece
        cols, _, w = span(piece)
        last = c == parts[k] - 1
        flying["gather", 0, piece].wait_recv()
        if last:
            total = jnp.sum(amp[k - 1, :, width - 128:], axis=0, keepdims=True)
            psend[k - 1] = jnp.broadcast_to(total[:, 127:128], (8, 128))
            final.append(push(psend.at[k - 1], precv.at[k - 1], {"occ": occ_at(k)}))
        hi, low = split(amp[k - 1, :, cols])
        t = dot(jnp.concatenate([hi, low], axis=0), bhi[cols, :])
        part = t[:VB] + t[VB:] + dot(hi, blo[cols, :])
        gsend[k - 1] = part if c == 0 else gsend[k - 1] + part
        if last:
            final.append(push(gsend.at[k - 1], grecv.at[k - 1], {"occ": occ_at(k)}))

    run = {"products": products, "reduce": reduce_level, "amplitudes": amplitudes,
           "gather": gather_level, "gammas": gammas}
    for stage, level, piece in schedule(levels, parts):
        run[stage](level, piece)

    for copy in final:
        copy.wait_recv()
    lane = lax.broadcasted_iota(jnp.int32, (8, 128), 1)
    eout[...] = jnp.where(lane == 0, precv[0], precv[1])[0:1, 0:2]
    gout[...] = grecv[0] + grecv[1]
    for copy, when in sends:
        if when is None:
            copy.wait_send()
        else:
            pl.when(when)(copy.wait_send)


def body(n, m, b_tensor, eps_occ, eps_virt):
    _, depth, nv = b_tensor.shape
    width = (nv // 128 + 1) * 128
    levels = m.bit_length() - 1
    offs = set(near(n, 1) + near(n, 2))
    ne = len(offs)
    tiles = width // 128
    parts = {k: p if tiles % p == 0 else 1 for k, p in PARTS.items()}
    rows = VB >> levels
    scratch = [
        pltpu.VMEM((width, depth), F32),
        pltpu.VMEM((width, depth), BF16),
        pltpu.VMEM((width, depth), BF16),
        pltpu.VMEM((ne, VB, depth), F32),
        pltpu.VMEM((4 * VB, depth), BF16),
        pltpu.VMEM((1, width), F32),
        pltpu.VMEM((128, 128), F32),
        pltpu.VMEM((8, 128), F32),
        pltpu.VMEM((2, 8, 128), F32),
        pltpu.VMEM((2, VB, width), F32),
        pltpu.VMEM((2, rows, width), F32),
        pltpu.VMEM((2, rows, 128), F32),
        pltpu.VMEM((2, VB, depth), F32),
        pltpu.VMEM((2, VB, depth), F32),
        pltpu.VMEM((2, 8, 128), F32),
        pltpu.VMEM((2, 8, 128), F32),
    ]
    for k in (1, 2):
        blocks = len(near(n, k))
        scratch += [pltpu.VMEM((blocks, VB >> level, width), F32) for level in range(levels + 1)]
        scratch += [pltpu.VMEM((blocks, VB >> (level + 1), width), F32) for level in range(levels)]
    copies = ne + 8 + (parts[1] + parts[2]) * (2 * levels + 1)
    scratch += [
        pltpu.SemaphoreType.DMA((1,)),
        pltpu.SemaphoreType.DMA((copies,)),
        pltpu.SemaphoreType.DMA((ne + copies,)),
    ]
    flops = 6 * depth * width * VB * (ne + 2)
    gamma, energy = pl.pallas_call(
        functools.partial(kernel, n, levels, parts, nv),
        out_shape=(jax.ShapeDtypeStruct((VB, depth), F32), jax.ShapeDtypeStruct((1, 2), F32)),
        in_specs=[
            pl.BlockSpec(memory_space=pl.ANY),
            pl.BlockSpec(memory_space=pltpu.SMEM),
            pl.BlockSpec(memory_space=pltpu.VMEM),
        ],
        out_specs=(pl.BlockSpec(memory_space=pltpu.VMEM), pl.BlockSpec(memory_space=pltpu.VMEM)),
        scratch_shapes=scratch,
        compiler_params=pltpu.CompilerParams(
            collective_id=0, has_side_effects=True, vmem_limit_bytes=VMEM_MIB * 2 ** 20),
        cost_estimate=pl.CostEstimate(flops=flops, bytes_accessed=4 * depth * nv, transcendentals=0),
    )(jnp.swapaxes(b_tensor, 1, 2), eps_occ, eps_virt.reshape(1, nv))
    return gamma.T[None], energy


def solution(mesh):
    placed = (P(("groups", "occ"), "aux", None), P(("groups", "occ")), P("groups"))
    return jax.shard_map(
        functools.partial(body, mesh.shape["occ"], mesh.shape["aux"]),
        mesh=mesh,
        in_specs=placed,
        out_specs=(P(("groups", "occ"), "aux", None), P(("groups", "occ"), None)),
        check_vma=False,
    )
```

```python
import functools

import jax
import jax.numpy as jnp
from jax import lax
from jax.experimental import pallas as pl
from jax.experimental.pallas import tpu as pltpu
from jax.sharding import PartitionSpec as P

VB = 64
HALVES = 2
VMEM_MIB = 60
MESH = pl.DeviceIdType.MESH
F32 = jnp.float32
BF16 = jnp.bfloat16


def split(x):
    hi = x.astype(BF16)
    return hi, (x - hi.astype(F32)).astype(BF16)


def dot(x, y):
    return lax.dot_general(x, y, (((1,), (0,)), ((), ())), preferred_element_type=F32)


def dot_t(x, y):
    return lax.dot_general(x, y, (((1,), (1,)), ((), ())), preferred_element_type=F32)


def near(n, k):
    return sorted({k % n, (n - k) % n})


def schedule(levels, halves):
    pieces = [(k, h) for h in range(halves) for k in (2, 1)]
    stages = [("products", 0)] + [("reduce", level) for level in range(levels)] + [("amplitudes", 0)]
    stages += [("gather", level) for level in range(levels - 1, 0, -1)] + [("gammas", 0)]
    order = []
    for t in range(len(pieces) + len(stages) - 1):
        for s in reversed(range(len(stages))):
            if 0 <= t - s < len(pieces):
                order.append((*stages[s], pieces[t - s]))
    return order


def kernel(n, levels, halves, nv, *refs):
    b_hbm, eo_ref, ev_ref, gout, eout = refs[:5]
    (bv, bhi, blo, srecv, ahi, evp, evc, esend, eocc, amp, ex,
     gsend, grecv, psend, precv) = refs[5:20]
    at = 20
    cur, rec = {}, {}
    for k in (1, 2):
        cur[k] = refs[at:at + levels + 1]
        rec[k] = refs[at + levels + 1:at + 2 * levels + 1]
        at += 2 * levels + 1
    load_sem, send_sem, recv_sem = refs[at:]

    offs = sorted(set(near(n, 1) + near(n, 2)))
    ne = len(offs)
    width, depth = bhi.shape
    me = lax.axis_index("occ")
    aux = lax.axis_index("aux")
    bits = [lax.rem(lax.div(aux, 2 ** level), 2) for level in range(levels)]
    buddy = [aux + (1 - 2 * bits[level]) * 2 ** level for level in range(levels)]
    part = VB // halves
    rows = part >> levels

    starts = []
    lo = 0
    for level in range(levels):
        lo = lo + bits[level] * (part >> (level + 1))
        starts.append(pl.multiple_of(lo, 8))
    lo = starts[-1]

    sends = []

    def occ_at(offset):
        return lax.rem(me + offset, n)

    def push(src, dst, target, slot=None, when=None):
        k = len(sends)
        copy = pltpu.make_async_remote_copy(
            src_ref=src, dst_ref=dst, send_sem=send_sem.at[k],
            recv_sem=recv_sem.at[ne * halves + k if slot is None else slot],
            device_id=target, device_id_type=MESH)
        if when is None:
            copy.start()
        else:
            pl.when(when)(copy.start)
        sends.append((copy, when))
        return copy

    barrier = pltpu.get_barrier_semaphore()
    for offset in offs:
        pl.semaphore_signal(barrier, inc=1, device_id={"occ": occ_at(offset)}, device_id_type=MESH)
    for level in range(levels):
        pl.semaphore_signal(barrier, inc=1, device_id={"aux": buddy[level]}, device_id_type=MESH)
    load = pltpu.make_async_copy(b_hbm.at[0], bv.at[pl.ds(0, nv), :], load_sem.at[0])
    load.start()
    esend[...] = jnp.full((8, 128), eo_ref[0], F32)
    pl.semaphore_wait(barrier, ne + levels)

    arrivals = {}

    def share(offset, h, when=None):
        slot = offs.index(offset)
        block = pl.ds(h * part, part)
        arrivals[offset, h] = push(
            b_hbm.at[0, block, :], srecv.at[slot, block, :], {"occ": occ_at(n - offset)},
            slot * halves + h, when)

    def share_all(h):
        for offset in near(n, 2):
            share(offset, h)
        if n == 4:
            share(1, h, me > 0)
            share(3, h, me < 3)
        else:
            for offset in near(n, 1):
                share(offset, h)

    def pass_on(h):
        if n == 4:
            arrivals[2, h].wait_recv()
            block = pl.ds(h * part, part)
            for offset, middle in ((1, 2), (3, 1)):
                slot = offs.index(offset)
                push(srecv.at[offs.index(2), block, :], srecv.at[slot, block, :],
                     {"occ": occ_at(offset)}, slot * halves + h, me == middle)

    share_all(0)
    e_copies = [push(esend, eocc.at[k - 1], {"occ": occ_at(n - k)}) for k in (2, 1)]

    evp[...] = jnp.ones_like(evp)
    evp[:, :nv] = ev_ref[...]
    evc[...] = jnp.broadcast_to(evp[:, :128], (128, 128)).T
    bv[nv:, :] = jnp.zeros((width - nv, depth), F32)
    load.wait()

    @pl.loop(0, width // 16)
    def _(t):
        block = pl.ds(pl.multiple_of(t * 16, 16), 16)
        hi, low = split(bv[block, :])
        bhi[block, :] = hi
        blo[block, :] = low

    pass_on(0)
    for h in range(1, halves):
        share_all(h)

    flying = {}

    def start_level(level, piece):
        k, h = piece
        half = part >> (level + 1)
        away = pl.multiple_of((1 - bits[level]) * half, 8)
        flying["reduce", level, piece] = push(
            cur[k][level].at[h, :, pl.ds(away, half), :], rec[k][level].at[h],
            {"aux": buddy[level]})

    def start_gather(level, piece):
        k, h = piece
        block = amp.at[k - 1, h, pl.ds(starts[level], part >> (level + 1)), :]
        flying["gather", level, piece] = push(block, block, {"aux": buddy[level]})

    def products(_, piece):
        k, h = piece
        mine = near(n, k)
        m = len(mine) * part
        if k == 2 and h > 0:
            pass_on(h)
        for s, offset in enumerate(mine):
            if not (n == 4 and offset == 2):
                arrivals[offset, h].wait_recv()
            hi, low = split(srecv[offs.index(offset), h * part:(h + 1) * part, :])
            ahi[s * part:(s + 1) * part, :] = hi
            ahi[m + s * part:m + (s + 1) * part, :] = low
        t = dot_t(ahi[:2 * m, :], bhi[...])
        u = dot_t(ahi[:m, :], blo[...])
        cur[k][0][h] = (t[:m] + t[m:] + u).reshape(len(mine), part, width)
        start_level(0, piece)

    def reduce_level(level, piece):
        k, h = piece
        half = part >> (level + 1)
        flying["reduce", level, piece].wait_recv()
        keep = pl.multiple_of(bits[level] * half, 8)
        cur[k][level + 1][h] = cur[k][level][h, :, pl.ds(keep, half), :] + rec[k][level][h]
        if level + 1 < levels:
            start_level(level + 1, piece)
        else:
            flying["ex", piece] = push(
                cur[k][levels].at[h, near(n, k).index(n - k)], ex.at[k - 1, h],
                {"occ": occ_at(n - k)})

    def amplitudes(_, piece):
        k, h = piece
        if h == 0:
            e_copies[2 - k].wait_recv()
        flying["ex", piece].wait_recv()
        coul = cur[k][levels][h, near(n, k).index(k)]
        exch = ex[k - 1, h]
        row = pl.multiple_of(h * part + lo, 8)
        base = evc[pl.ds(row, rows), 0:1] - eocc[k - 1, 0:1, 0:1] - esend[0:1, 0:1]
        val = (2.0 * coul - exch) / (base + evp[...])
        energy = jnp.sum(coul * val, axis=1, keepdims=True)
        column = lax.broadcasted_iota(jnp.int32, (rows, width), 1)
        amp[k - 1, h, pl.ds(lo, rows), :] = jnp.where(column < nv, val, energy)
        start_gather(levels - 1, piece)

    def gather_level(level, piece):
        flying["gather", level, piece].wait_recv()
        start_gather(level - 1, piece)

    final = []

    def gammas(_, piece):
        k, h = piece
        flying["gather", 0, piece].wait_recv()
        hi, low = split(amp[k - 1, h])
        t = dot(jnp.concatenate([hi, low], axis=0), bhi[...])
        gsend[k - 1, h] = t[:part] + t[part:] + dot(hi, blo[...])
        final.append(push(gsend.at[k - 1, h], grecv.at[k - 1, h], {"occ": occ_at(k)}))
        if h == halves - 1:
            ends = amp[k - 1, :, :, width - 128:].reshape(VB, 128)
            total = jnp.sum(ends, axis=0, keepdims=True)
            psend[k - 1] = jnp.broadcast_to(total[:, 127:128], (8, 128))
            final.append(push(psend.at[k - 1], precv.at[k - 1], {"occ": occ_at(k)}))

    run = {"products": products, "reduce": reduce_level, "amplitudes": amplitudes,
           "gather": gather_level, "gammas": gammas}
    for stage, level, piece in schedule(levels, halves):
        run[stage](level, piece)

    for copy in final:
        copy.wait_recv()
    lane = lax.broadcasted_iota(jnp.int32, (8, 128), 1)
    eout[...] = jnp.where(lane == 0, precv[0], precv[1])[0:1, 0:2]
    gout[...] = (grecv[0] + grecv[1]).reshape(VB, depth)
    for copy, when in sends:
        if when is None:
            copy.wait_send()
        else:
            pl.when(when)(copy.wait_send)


def body(n, m, b_tensor, eps_occ, eps_virt):
    _, depth, nv = b_tensor.shape
    width = (nv // 128 + 1) * 128
    levels = m.bit_length() - 1
    offs = set(near(n, 1) + near(n, 2))
    ne = len(offs)
    halves = HALVES if VB % (8 * HALVES * m) == 0 else 1
    part = VB // halves
    rows = part >> levels
    scratch = [
        pltpu.VMEM((width, depth), F32),
        pltpu.VMEM((width, depth), BF16),
        pltpu.VMEM((width, depth), BF16),
        pltpu.VMEM((ne, VB, depth), F32),
        pltpu.VMEM((4 * VB, depth), BF16),
        pltpu.VMEM((1, width), F32),
        pltpu.VMEM((128, 128), F32),
        pltpu.VMEM((8, 128), F32),
        pltpu.VMEM((2, 8, 128), F32),
        pltpu.VMEM((2, halves, part, width), F32),
        pltpu.VMEM((2, halves, rows, width), F32),
        pltpu.VMEM((2, halves, part, depth), F32),
        pltpu.VMEM((2, halves, part, depth), F32),
        pltpu.VMEM((2, 8, 128), F32),
        pltpu.VMEM((2, 8, 128), F32),
    ]
    for k in (1, 2):
        blocks = len(near(n, k))
        scratch += [pltpu.VMEM((halves, blocks, part >> level, width), F32) for level in range(levels + 1)]
        scratch += [pltpu.VMEM((halves, blocks, part >> (level + 1), width), F32) for level in range(levels)]
    copies = (ne + 4) * halves + 4 + 2 * halves * (2 * levels + 1)
    scratch += [
        pltpu.SemaphoreType.DMA((1,)),
        pltpu.SemaphoreType.DMA((copies,)),
        pltpu.SemaphoreType.DMA((ne * halves + copies,)),
    ]
    flops = 6 * depth * width * VB * (ne + 2)
    gamma, energy = pl.pallas_call(
        functools.partial(kernel, n, levels, halves, nv),
        out_shape=(jax.ShapeDtypeStruct((VB, depth), F32), jax.ShapeDtypeStruct((1, 2), F32)),
        in_specs=[
            pl.BlockSpec(memory_space=pl.ANY),
            pl.BlockSpec(memory_space=pltpu.SMEM),
            pl.BlockSpec(memory_space=pltpu.VMEM),
        ],
        out_specs=(pl.BlockSpec(memory_space=pltpu.VMEM), pl.BlockSpec(memory_space=pltpu.VMEM)),
        scratch_shapes=scratch,
        compiler_params=pltpu.CompilerParams(
            collective_id=0, has_side_effects=True, vmem_limit_bytes=VMEM_MIB * 2 ** 20),
        cost_estimate=pl.CostEstimate(flops=flops, bytes_accessed=4 * depth * nv, transcendentals=0),
    )(jnp.swapaxes(b_tensor, 1, 2), eps_occ, eps_virt.reshape(1, nv))
    return gamma.T[None], energy


def solution(mesh):
    placed = (P(("groups", "occ"), "aux", None), P(("groups", "occ")), P("groups"))
    return jax.shard_map(
        functools.partial(body, mesh.shape["occ"], mesh.shape["aux"]),
        mesh=mesh,
        in_specs=placed,
        out_specs=(P(("groups", "occ"), "aux", None), P(("groups", "occ"), None)),
        check_vma=False,
    )
```

```python
import functools

import jax
import jax.numpy as jnp
from jax import lax
from jax.experimental import pallas as pl
from jax.experimental.pallas import tpu as pltpu
from jax.sharding import PartitionSpec as P

VB = 64
HALVES = 2
VMEM_MIB = 52
MESH = pl.DeviceIdType.MESH
F32 = jnp.float32
BF16 = jnp.bfloat16


def split(x):
    hi = x.astype(BF16)
    return hi, (x - hi.astype(F32)).astype(BF16)


def dot(x, y):
    return lax.dot_general(x, y, (((1,), (0,)), ((), ())), preferred_element_type=F32)


def dot_t(x, y):
    return lax.dot_general(x, y, (((1,), (1,)), ((), ())), preferred_element_type=F32)


def near(n, k):
    return sorted({k % n, (n - k) % n})


def schedule(levels, halves):
    pieces = [(k, h) for h in range(halves) for k in (2, 1)]
    stages = [("products", 0)] + [("reduce", level) for level in range(levels)] + [("amplitudes", 0)]
    stages += [("gather", level) for level in range(levels - 1, 0, -1)] + [("gammas", 0)]
    order = []
    for t in range(len(pieces) + len(stages) - 1):
        for s in reversed(range(len(stages))):
            if 0 <= t - s < len(pieces):
                order.append((*stages[s], pieces[t - s]))
    return order


def kernel(n, levels, halves, nv, *refs):
    b_hbm, eo_ref, ev_ref, gout, eout = refs[:5]
    (bv, bhi, blo, srecv, ahi, evp, evc, esend, eocc, amp, ex,
     gsend, grecv, psend, precv) = refs[5:20]
    at = 20
    cur, rec = {}, {}
    for k in (1, 2):
        cur[k] = refs[at:at + levels + 1]
        rec[k] = refs[at + levels + 1:at + 2 * levels + 1]
        at += 2 * levels + 1
    load_sem, send_sem, recv_sem = refs[at:]

    offs = sorted(set(near(n, 1) + near(n, 2)))
    ne = len(offs)
    width, depth = bhi.shape
    me = lax.axis_index("occ")
    aux = lax.axis_index("aux")
    bits = [lax.rem(lax.div(aux, 2 ** level), 2) for level in range(levels)]
    buddy = [aux + (1 - 2 * bits[level]) * 2 ** level for level in range(levels)]
    part = VB // halves
    rows = part >> levels

    starts = []
    lo = 0
    for level in range(levels):
        lo = lo + bits[level] * (part >> (level + 1))
        starts.append(pl.multiple_of(lo, 8))
    lo = starts[-1]

    sends = []

    def occ_at(offset):
        return lax.rem(me + offset, n)

    def push(src, dst, target, slot=None, when=None):
        k = len(sends)
        copy = pltpu.make_async_remote_copy(
            src_ref=src, dst_ref=dst, send_sem=send_sem.at[k],
            recv_sem=recv_sem.at[ne * halves + k if slot is None else slot],
            device_id=target, device_id_type=MESH)
        if when is None:
            copy.start()
        else:
            pl.when(when)(copy.start)
        sends.append((copy, when))
        return copy

    barrier = pltpu.get_barrier_semaphore()
    for offset in offs:
        pl.semaphore_signal(barrier, inc=1, device_id={"occ": occ_at(offset)}, device_id_type=MESH)
    for level in range(levels):
        pl.semaphore_signal(barrier, inc=1, device_id={"aux": buddy[level]}, device_id_type=MESH)
    load = pltpu.make_async_copy(b_hbm.at[0], bv.at[pl.ds(0, nv), :], load_sem.at[0])
    load.start()
    esend[...] = jnp.full((8, 128), eo_ref[0], F32)
    pl.semaphore_wait(barrier, ne + levels)

    arrivals = {}

    def share(offset, h, when=None):
        slot = offs.index(offset)
        block = pl.ds(h * part, part)
        arrivals[offset, h] = push(
            b_hbm.at[0, block, :], srecv.at[slot, block, :], {"occ": occ_at(n - offset)},
            slot * halves + h, when)

    def share_all(h):
        for offset in near(n, 2):
            share(offset, h)
        if n == 4:
            share(1, h, me > 0)
            share(3, h, me < 3)
        else:
            for offset in near(n, 1):
                share(offset, h)

    def pass_on(h):
        if n == 4:
            arrivals[2, h].wait_recv()
            block = pl.ds(h * part, part)
            for offset, middle in ((1, 2), (3, 1)):
                slot = offs.index(offset)
                push(srecv.at[offs.index(2), block, :], srecv.at[slot, block, :],
                     {"occ": occ_at(offset)}, slot * halves + h, me == middle)

    share_all(0)
    e_copies = [push(esend, eocc.at[k - 1], {"occ": occ_at(n - k)}) for k in (2, 1)]

    evp[...] = jnp.ones_like(evp)
    evp[:, :nv] = ev_ref[...]
    evc[...] = jnp.broadcast_to(evp[:, :128], (128, 128)).T
    bv[nv:, :] = jnp.zeros((width - nv, depth), F32)
    load.wait()

    @pl.loop(0, width // 16)
    def _(t):
        block = pl.ds(pl.multiple_of(t * 16, 16), 16)
        hi, low = split(bv[block, :])
        bhi[block, :] = hi
        blo[block, :] = low

    pass_on(0)
    for h in range(1, halves):
        share_all(h)

    flying = {}

    def start_level(level, piece):
        k, h = piece
        half = part >> (level + 1)
        away = pl.multiple_of((1 - bits[level]) * half, 8)
        flying["reduce", level, piece] = push(
            cur[k][level].at[h, :, pl.ds(away, half), :], rec[k][level].at[h],
            {"aux": buddy[level]})

    def start_gather(level, piece):
        k, h = piece
        block = amp.at[k - 1, h, pl.ds(starts[level], part >> (level + 1)), :]
        flying["gather", level, piece] = push(block, block, {"aux": buddy[level]})

    def products(_, piece):
        k, h = piece
        mine = near(n, k)
        m = len(mine) * part
        if k == 2 and h > 0:
            pass_on(h)
        for s, offset in enumerate(mine):
            if not (n == 4 and offset == 2):
                arrivals[offset, h].wait_recv()
            hi, low = split(srecv[offs.index(offset), h * part:(h + 1) * part, :])
            ahi[s * part:(s + 1) * part, :] = hi
            ahi[m + s * part:m + (s + 1) * part, :] = low
        t = dot_t(ahi[:2 * m, :], bhi[...])
        u = dot_t(ahi[:m, :], blo[...])
        cur[k][0][h] = (t[:m] + t[m:] + u).reshape(len(mine), part, width)
        start_level(0, piece)

    def reduce_level(level, piece):
        k, h = piece
        half = part >> (level + 1)
        flying["reduce", level, piece].wait_recv()
        keep = pl.multiple_of(bits[level] * half, 8)
        cur[k][level + 1][h] = cur[k][level][h, :, pl.ds(keep, half), :] + rec[k][level][h]
        if level + 1 < levels:
            start_level(level + 1, piece)
        else:
            flying["ex", piece] = push(
                cur[k][levels].at[h, near(n, k).index(n - k)], ex.at[k - 1, h],
                {"occ": occ_at(n - k)})

    def amplitudes(_, piece):
        k, h = piece
        if h == 0:
            e_copies[2 - k].wait_recv()
        flying["ex", piece].wait_recv()
        coul = cur[k][levels][h, near(n, k).index(k)]
        exch = ex[k - 1, h]
        row = pl.multiple_of(h * part + lo, 8)
        base = evc[pl.ds(row, rows), 0:1] - eocc[k - 1, 0:1, 0:1] - esend[0:1, 0:1]
        val = (2.0 * coul - exch) / (base + evp[...])
        energy = jnp.sum(coul * val, axis=1, keepdims=True)
        column = lax.broadcasted_iota(jnp.int32, (rows, width), 1)
        amp[k - 1, h, pl.ds(lo, rows), :] = jnp.where(column < nv, val, energy)
        start_gather(levels - 1, piece)

    def gather_level(level, piece):
        flying["gather", level, piece].wait_recv()
        start_gather(level - 1, piece)

    final = []

    def gammas(_, piece):
        k, h = piece
        flying["gather", 0, piece].wait_recv()
        hi, low = split(amp[k - 1, h])
        t = dot(jnp.concatenate([hi, low], axis=0), bhi[...])
        gsend[k - 1, h] = t[:part] + t[part:] + dot(hi, blo[...])
        final.append(push(gsend.at[k - 1, h], grecv.at[k - 1, h], {"occ": occ_at(k)}))
        if h == halves - 1:
            ends = amp[k - 1, :, :, width - 128:].reshape(VB, 128)
            total = jnp.sum(ends, axis=0, keepdims=True)
            psend[k - 1] = jnp.broadcast_to(total[:, 127:128], (8, 128))
            final.append(push(psend.at[k - 1], precv.at[k - 1], {"occ": occ_at(k)}))

    run = {"products": products, "reduce": reduce_level, "amplitudes": amplitudes,
           "gather": gather_level, "gammas": gammas}
    for stage, level, piece in schedule(levels, halves):
        run[stage](level, piece)

    for copy in final:
        copy.wait_recv()
    lane = lax.broadcasted_iota(jnp.int32, (8, 128), 1)
    eout[...] = jnp.where(lane == 0, precv[0], precv[1])[0:1, 0:2]
    gout[...] = (grecv[0] + grecv[1]).reshape(VB, depth)
    for copy, when in sends:
        if when is None:
            copy.wait_send()
        else:
            pl.when(when)(copy.wait_send)


def body(n, m, b_tensor, eps_occ, eps_virt):
    _, depth, nv = b_tensor.shape
    width = (nv // 128 + 1) * 128
    levels = m.bit_length() - 1
    offs = set(near(n, 1) + near(n, 2))
    ne = len(offs)
    halves = HALVES if VB % (8 * HALVES * m) == 0 else 1
    part = VB // halves
    rows = part >> levels
    scratch = [
        pltpu.VMEM((width, depth), F32),
        pltpu.VMEM((width, depth), BF16),
        pltpu.VMEM((width, depth), BF16),
        pltpu.VMEM((ne, VB, depth), F32),
        pltpu.VMEM((4 * VB, depth), BF16),
        pltpu.VMEM((1, width), F32),
        pltpu.VMEM((128, 128), F32),
        pltpu.VMEM((8, 128), F32),
        pltpu.VMEM((2, 8, 128), F32),
        pltpu.VMEM((2, halves, part, width), F32),
        pltpu.VMEM((2, halves, rows, width), F32),
        pltpu.VMEM((2, halves, part, depth), F32),
        pltpu.VMEM((2, halves, part, depth), F32),
        pltpu.VMEM((2, 8, 128), F32),
        pltpu.VMEM((2, 8, 128), F32),
    ]
    for k in (1, 2):
        blocks = len(near(n, k))
        scratch += [pltpu.VMEM((halves, blocks, part >> level, width), F32) for level in range(levels + 1)]
        scratch += [pltpu.VMEM((halves, blocks, part >> (level + 1), width), F32) for level in range(levels)]
    copies = (ne + 4) * halves + 4 + 2 * halves * (2 * levels + 1)
    scratch += [
        pltpu.SemaphoreType.DMA((1,)),
        pltpu.SemaphoreType.DMA((copies,)),
        pltpu.SemaphoreType.DMA((ne * halves + copies,)),
    ]
    flops = 6 * depth * width * VB * (ne + 2)
    gamma, energy = pl.pallas_call(
        functools.partial(kernel, n, levels, halves, nv),
        out_shape=(jax.ShapeDtypeStruct((VB, depth), F32), jax.ShapeDtypeStruct((1, 2), F32)),
        in_specs=[
            pl.BlockSpec(memory_space=pl.ANY),
            pl.BlockSpec(memory_space=pltpu.SMEM),
            pl.BlockSpec(memory_space=pltpu.VMEM),
        ],
        out_specs=(pl.BlockSpec(memory_space=pltpu.VMEM), pl.BlockSpec(memory_space=pltpu.VMEM)),
        scratch_shapes=scratch,
        compiler_params=pltpu.CompilerParams(
            collective_id=0, has_side_effects=True, vmem_limit_bytes=VMEM_MIB * 2 ** 20),
        cost_estimate=pl.CostEstimate(flops=flops, bytes_accessed=4 * depth * nv, transcendentals=0),
    )(jnp.swapaxes(b_tensor, 1, 2), eps_occ, eps_virt.reshape(1, nv))
    return gamma.T[None], energy


def solution(mesh):
    placed = (P(("groups", "occ"), "aux", None), P(("groups", "occ")), P("groups"))
    return jax.shard_map(
        functools.partial(body, mesh.shape["occ"], mesh.shape["aux"]),
        mesh=mesh,
        in_specs=placed,
        out_specs=(P(("groups", "occ"), "aux", None), P(("groups", "occ"), None)),
        check_vma=False,
    )
```

```python
import functools

import jax
import jax.numpy as jnp
from jax import lax
from jax.experimental import pallas as pl
from jax.experimental.pallas import tpu as pltpu
from jax.sharding import PartitionSpec as P

VB = 64
HALVES = 2
VMEM_MIB = 52
MESH = pl.DeviceIdType.MESH
F32 = jnp.float32
BF16 = jnp.bfloat16


def split(x):
    hi = x.astype(BF16)
    return hi, (x - hi.astype(F32)).astype(BF16)


def dot(x, y):
    return lax.dot_general(x, y, (((1,), (0,)), ((), ())), preferred_element_type=F32)


def dot_t(x, y):
    return lax.dot_general(x, y, (((1,), (1,)), ((), ())), preferred_element_type=F32)


def near(n, k):
    return sorted({k % n, (n - k) % n})


def schedule(levels, halves):
    pieces = [(k, h) for h in range(halves) for k in (2, 1)]
    stages = [("products", 0)] + [("reduce", level) for level in range(levels)] + [("amplitudes", 0)]
    stages += [("gather", level) for level in range(levels - 1, 0, -1)] + [("gammas", 0)]
    order = []
    for t in range(len(pieces) + len(stages) - 1):
        for s in reversed(range(len(stages))):
            if 0 <= t - s < len(pieces):
                order.append((*stages[s], pieces[t - s]))
    return order


def kernel(n, levels, halves, nv, *refs):
    b_hbm, eo_ref, ev_ref, gout, eout = refs[:5]
    (bv, bhi, blo, srecv, ahi, evp, evc, esend, eocc, amp, ex,
     gsend, grecv, psend, precv) = refs[5:20]
    at = 20
    cur, rec = {}, {}
    for k in (1, 2):
        cur[k] = refs[at:at + levels + 1]
        rec[k] = refs[at + levels + 1:at + 2 * levels + 1]
        at += 2 * levels + 1
    load_sem, send_sem, recv_sem = refs[at:]

    offs = sorted(set(near(n, 1) + near(n, 2)))
    ne = len(offs)
    width, depth = bhi.shape
    me = lax.axis_index("occ")
    aux = lax.axis_index("aux")
    bits = [lax.rem(lax.div(aux, 2 ** level), 2) for level in range(levels)]
    buddy = [aux + (1 - 2 * bits[level]) * 2 ** level for level in range(levels)]
    part = VB // halves
    rows = part >> levels

    starts = []
    lo = 0
    for level in range(levels):
        lo = lo + bits[level] * (part >> (level + 1))
        starts.append(pl.multiple_of(lo, 8))
    lo = starts[-1]

    sends = []

    def occ_at(offset):
        return lax.rem(me + offset, n)

    def push(src, dst, target, slot=None, when=None):
        k = len(sends)
        copy = pltpu.make_async_remote_copy(
            src_ref=src, dst_ref=dst, send_sem=send_sem.at[k],
            recv_sem=recv_sem.at[ne * halves + k if slot is None else slot],
            device_id=target, device_id_type=MESH)
        if when is None:
            copy.start()
        else:
            pl.when(when)(copy.start)
        sends.append((copy, when))
        return copy

    barrier = pltpu.get_barrier_semaphore()
    for offset in offs:
        pl.semaphore_signal(barrier, inc=1, device_id={"occ": occ_at(offset)}, device_id_type=MESH)
    for level in range(levels):
        pl.semaphore_signal(barrier, inc=1, device_id={"aux": buddy[level]}, device_id_type=MESH)
    load = pltpu.make_async_copy(b_hbm.at[0], bv.at[pl.ds(0, nv), :], load_sem.at[0])
    load.start()
    esend[...] = jnp.full((8, 128), eo_ref[0], F32)
    pl.semaphore_wait(barrier, ne + levels)

    arrivals = {}

    def share(offset, h, when=None):
        slot = offs.index(offset)
        block = pl.ds(h * part, part)
        arrivals[offset, h] = push(
            b_hbm.at[0, block, :], srecv.at[slot, block, :], {"occ": occ_at(n - offset)},
            slot * halves + h, when)

    def share_all(h):
        for offset in near(n, 2):
            share(offset, h)
        if n == 4:
            share(1, h, me > 0)
            share(3, h, me < 3)
        else:
            for offset in near(n, 1):
                share(offset, h)

    def pass_on(h):
        if n == 4:
            arrivals[2, h].wait_recv()
            block = pl.ds(h * part, part)
            for offset, middle in ((1, 2), (3, 1)):
                slot = offs.index(offset)
                push(srecv.at[offs.index(2), block, :], srecv.at[slot, block, :],
                     {"occ": occ_at(offset)}, slot * halves + h, me == middle)

    share_all(0)
    e_copies = [push(esend, eocc.at[k - 1], {"occ": occ_at(n - k)}) for k in (2, 1)]

    evp[...] = jnp.ones_like(evp)
    evp[:, :nv] = ev_ref[...]
    evc[...] = jnp.broadcast_to(evp[:, :128], (128, 128)).T
    bv[nv:, :] = jnp.zeros((width - nv, depth), F32)
    load.wait()

    @pl.loop(0, width // 16)
    def _(t):
        block = pl.ds(pl.multiple_of(t * 16, 16), 16)
        hi, low = split(bv[block, :])
        bhi[block, :] = hi
        blo[block, :] = low

    pass_on(0)
    for h in range(1, halves):
        share_all(h)

    flying = {}

    def start_level(level, piece):
        k, h = piece
        half = part >> (level + 1)
        away = pl.multiple_of((1 - bits[level]) * half, 8)
        flying["reduce", level, piece] = push(
            cur[k][level].at[h, :, pl.ds(away, half), :], rec[k][level].at[h],
            {"aux": buddy[level]})

    def start_gather(level, piece):
        k, h = piece
        block = amp.at[k - 1, h, pl.ds(starts[level], part >> (level + 1)), :]
        flying["gather", level, piece] = push(block, block, {"aux": buddy[level]})

    def products(_, piece):
        k, h = piece
        mine = near(n, k)
        m = len(mine) * part
        if k == 2 and h > 0:
            pass_on(h)
        for s, offset in enumerate(mine):
            if not (n == 4 and offset == 2):
                arrivals[offset, h].wait_recv()
            hi, low = split(srecv[offs.index(offset), h * part:(h + 1) * part, :])
            ahi[s * part:(s + 1) * part, :] = hi
            ahi[m + s * part:m + (s + 1) * part, :] = low
        t = dot_t(ahi[:2 * m, :], bhi[...])
        u = dot_t(ahi[:m, :], blo[...])
        cur[k][0][h] = (t[:m] + t[m:] + u).reshape(len(mine), part, width)
        start_level(0, piece)

    def reduce_level(level, piece):
        k, h = piece
        half = part >> (level + 1)
        flying["reduce", level, piece].wait_recv()
        keep = pl.multiple_of(bits[level] * half, 8)
        cur[k][level + 1][h] = cur[k][level][h, :, pl.ds(keep, half), :] + rec[k][level][h]
        if level + 1 < levels:
            start_level(level + 1, piece)
        else:
            flying["ex", piece] = push(
                cur[k][levels].at[h, near(n, k).index(n - k)], ex.at[k - 1, h],
                {"occ": occ_at(n - k)})

    def amplitudes(_, piece):
        k, h = piece
        if h == 0:
            e_copies[2 - k].wait_recv()
        flying["ex", piece].wait_recv()
        coul = cur[k][levels][h, near(n, k).index(k)]
        exch = ex[k - 1, h]
        row = pl.multiple_of(h * part + lo, 8)
        base = evc[pl.ds(row, rows), 0:1] - eocc[k - 1, 0:1, 0:1] - esend[0:1, 0:1]
        val = (2.0 * coul - exch) / (base + evp[...])
        energy = jnp.sum(coul * val, axis=1, keepdims=True)
        column = lax.broadcasted_iota(jnp.int32, (rows, width), 1)
        amp[k - 1, h, pl.ds(lo, rows), :] = jnp.where(column < nv, val, energy)
        start_gather(levels - 1, piece)

    def gather_level(level, piece):
        flying["gather", level, piece].wait_recv()
        start_gather(level - 1, piece)

    final = []
    between = {}

    def gammas(_, piece):
        k, h = piece
        flying["gather", 0, piece].wait_recv()
        hi, low = split(amp[k - 1, h])
        t = dot(jnp.concatenate([hi, low], axis=0), bhi[...])
        value = t[:part] + t[part:] + dot(hi, blo[...])
        if k == 2:
            gsend[1, h] = value
            between[h] = push(gsend.at[1, h], grecv.at[1, h], {"occ": occ_at(1)})
        else:
            between[h].wait_recv()
            gsend[0, h] = value + grecv[1, h]
            final.append(push(gsend.at[0, h], grecv.at[0, h], {"occ": occ_at(1)}))
        if h == halves - 1:
            ends = amp[k - 1, :, :, width - 128:].reshape(VB, 128)
            total = jnp.sum(ends, axis=0, keepdims=True)
            psend[k - 1] = jnp.broadcast_to(total[:, 127:128], (8, 128))
            final.append(push(psend.at[k - 1], precv.at[k - 1], {"occ": occ_at(k)}))

    run = {"products": products, "reduce": reduce_level, "amplitudes": amplitudes,
           "gather": gather_level, "gammas": gammas}
    for stage, level, piece in schedule(levels, halves):
        run[stage](level, piece)

    for copy in final:
        copy.wait_recv()
    lane = lax.broadcasted_iota(jnp.int32, (8, 128), 1)
    eout[...] = jnp.where(lane == 0, precv[0], precv[1])[0:1, 0:2]
    gout[...] = grecv[0].reshape(VB, depth)
    for copy, when in sends:
        if when is None:
            copy.wait_send()
        else:
            pl.when(when)(copy.wait_send)


def body(n, m, b_tensor, eps_occ, eps_virt):
    _, depth, nv = b_tensor.shape
    width = (nv // 128 + 1) * 128
    levels = m.bit_length() - 1
    offs = set(near(n, 1) + near(n, 2))
    ne = len(offs)
    halves = HALVES if VB % (8 * HALVES * m) == 0 else 1
    part = VB // halves
    rows = part >> levels
    scratch = [
        pltpu.VMEM((width, depth), F32),
        pltpu.VMEM((width, depth), BF16),
        pltpu.VMEM((width, depth), BF16),
        pltpu.VMEM((ne, VB, depth), F32),
        pltpu.VMEM((4 * VB, depth), BF16),
        pltpu.VMEM((1, width), F32),
        pltpu.VMEM((128, 128), F32),
        pltpu.VMEM((8, 128), F32),
        pltpu.VMEM((2, 8, 128), F32),
        pltpu.VMEM((2, halves, part, width), F32),
        pltpu.VMEM((2, halves, rows, width), F32),
        pltpu.VMEM((2, halves, part, depth), F32),
        pltpu.VMEM((2, halves, part, depth), F32),
        pltpu.VMEM((2, 8, 128), F32),
        pltpu.VMEM((2, 8, 128), F32),
    ]
    for k in (1, 2):
        blocks = len(near(n, k))
        scratch += [pltpu.VMEM((halves, blocks, part >> level, width), F32) for level in range(levels + 1)]
        scratch += [pltpu.VMEM((halves, blocks, part >> (level + 1), width), F32) for level in range(levels)]
    copies = (ne + 4) * halves + 4 + 2 * halves * (2 * levels + 1)
    scratch += [
        pltpu.SemaphoreType.DMA((1,)),
        pltpu.SemaphoreType.DMA((copies,)),
        pltpu.SemaphoreType.DMA((ne * halves + copies,)),
    ]
    flops = 6 * depth * width * VB * (ne + 2)
    gamma, energy = pl.pallas_call(
        functools.partial(kernel, n, levels, halves, nv),
        out_shape=(jax.ShapeDtypeStruct((VB, depth), F32), jax.ShapeDtypeStruct((1, 2), F32)),
        in_specs=[
            pl.BlockSpec(memory_space=pl.ANY),
            pl.BlockSpec(memory_space=pltpu.SMEM),
            pl.BlockSpec(memory_space=pltpu.VMEM),
        ],
        out_specs=(pl.BlockSpec(memory_space=pltpu.VMEM), pl.BlockSpec(memory_space=pltpu.VMEM)),
        scratch_shapes=scratch,
        compiler_params=pltpu.CompilerParams(
            collective_id=0, has_side_effects=True, vmem_limit_bytes=VMEM_MIB * 2 ** 20),
        cost_estimate=pl.CostEstimate(flops=flops, bytes_accessed=4 * depth * nv, transcendentals=0),
    )(jnp.swapaxes(b_tensor, 1, 2), eps_occ, eps_virt.reshape(1, nv))
    return gamma.T[None], energy


def solution(mesh):
    placed = (P(("groups", "occ"), "aux", None), P(("groups", "occ")), P("groups"))
    return jax.shard_map(
        functools.partial(body, mesh.shape["occ"], mesh.shape["aux"]),
        mesh=mesh,
        in_specs=placed,
        out_specs=(P(("groups", "occ"), "aux", None), P(("groups", "occ"), None)),
        check_vma=False,
    )
```
